32 devices in a mesh: pipe: 4 (over y, core), expert: 4 (over z), tensor: 2 (over x).
Axes of the slice: x: 2, y: 2, z: 4, core: 2. Of those that a mesh axis runs over, the one named last changes fastest.
Arguments:
- acts: bfloat16 [4, 2, 512, 2048], P('pipe', None, 'expert', 'tensor'), may hold values from -6 to 6
- out_grad: bfloat16 [4, 2, 512, 2048], P('pipe', None, 'expert', 'tensor'), may hold values from -4 to 4
- probs: bfloat16 [4, 2, 512], P('pipe', None, 'expert'), may hold values from 0.099609375 to 1
- counts: int32 [4, 2, 4, 4], P('pipe', None, 'expert'), may hold values from 1 to 64, as said below
- w_gate: bfloat16 [4, 4, 1024, 512], P('pipe', 'expert', None, 'tensor'), may hold values from -0.125 to 0.125
- w_up: bfloat16 [4, 4, 1024, 512], P('pipe', 'expert', None, 'tensor'), may hold values from -0.125 to 0.125
- w_down: bfloat16 [4, 4, 512, 1024], P('pipe', 'expert', 'tensor'), may hold values from -0.25 to 0.25
Outputs:
- act_grad: bfloat16 [4, 2, 512, 2048], P('pipe', None, 'expert', 'tensor')
- prob_grad: bfloat16 [4, 2, 512], P('pipe', None, 'expert')
- gate_grad: bfloat16 [4, 4, 1024, 512], P('pipe', 'expert', None, 'tensor')
- up_grad: bfloat16 [4, 4, 1024, 512], P('pipe', 'expert', None, 'tensor')
- down_grad: bfloat16 [4, 4, 512, 1024], P('pipe', 'expert', 'tensor')
The draws below stay inside these ranges and needn't reach their ends.
Inputs may be any that keep to these rules, and one draw needn't show every extreme that they name: Row [p, d, s] of counts sums to 128; for each section and direction one expert gets exactly 64 rows from every source; no count exceeds 64.
All inputs are finite; a program needn't handle non-finite values.
Results may differ from the reference program's by a relative error of at most 0.008.
Values may be sent and summed in bfloat16 or wider, within the bound.
A program may use at most 64 MiB of HBM per device.

```python
import jax
import jax.numpy as jnp
from jax import lax

D = 2048
FF = 512
ROWS = 128
EXPERTS = 4
CAP = 64
SECTION_ROWS = 512
N_PIPE = 4
N_EXPERT = 4


def draw_counts(key, part):
    base_key = jax.random.fold_in(key, 7)
    others = EXPERTS - 1
    pairs = others // 2
    spread = (ROWS - CAP) // others
    extra = ROWS - CAP - spread * others
    reach = max(spread - 1, 0)
    position = jnp.arange(others, dtype=jnp.int32)
    bases = spread + (position < extra).astype(jnp.int32)

    def one_source(section, direction, source):
        group_key = jax.random.fold_in(jax.random.fold_in(base_key, section), direction)
        order = jax.random.permutation(group_key, EXPERTS).astype(jnp.int32)
        own_key = jax.random.fold_in(group_key, source + 1000)
        shifts = jax.random.randint(own_key, (pairs,), -reach, reach + 1, dtype=jnp.int32)
        moves = jnp.zeros((others,), jnp.int32).at[:pairs].add(shifts).at[pairs:2 * pairs].add(-shifts)
        values = jnp.concatenate([jnp.full((1,), CAP, jnp.int32), bases + moves])
        return jnp.zeros((EXPERTS,), jnp.int32).at[order].set(values)
    sections = jnp.arange(N_PIPE, dtype=jnp.int32)
    directions = jnp.arange(2, dtype=jnp.int32)
    sources = jnp.arange(N_EXPERT, dtype=jnp.int32)
    over_source = jax.vmap(one_source, in_axes=(None, None, 0))
    over_direction = jax.vmap(over_source, in_axes=(None, 0, None))
    over_section = jax.vmap(over_direction, in_axes=(0, None, None))
    return over_section(sections, directions, sources)


def level_of(rng, dims, pieces, smallest, largest):
    level, own = 1.0, jax.random.fold_in(rng, 6)
    for axis_at, shards_of in pieces:
        steps = jnp.exp(jax.random.uniform(jax.random.fold_in(own, axis_at), (shards_of,), jnp.float32, smallest / len(pieces), largest / len(pieces)))
        level = level * jnp.repeat(steps, dims[axis_at] // shards_of).reshape([-1 if axis == axis_at else 1 for axis in range(len(dims))])
    return level


def centred(stream_key, dims, deviation, limit, split=(), kind=jnp.bfloat16):
    gain = level_of(stream_key, dims, split, -0.22, 0.18) if split else 1.0
    result = jax.random.normal(stream_key, dims, jnp.float32) * deviation * gain
    return jnp.minimum(jnp.maximum(result, -limit), limit).astype(kind)


def setup_inputs(seed: int = 0) -> dict:
    streams_of = jax.random.split(jax.random.key(seed), 8)
    acts = centred(streams_of[0], (N_PIPE, 2, SECTION_ROWS, D), 1.0, 6.0, ((0, 4), (2, 4), (3, 2)))
    out_grad = centred(streams_of[1], (N_PIPE, 2, SECTION_ROWS, D), 0.5, 4.0, ((0, 4), (2, 4), (3, 2)))
    probs = jnp.clip(0.099609375 + 0.9003906 * jax.random.uniform(streams_of[2], (N_PIPE, 2, SECTION_ROWS), jnp.float32) ** level_of(streams_of[2], (N_PIPE, 2, SECTION_ROWS), ((0, 4), (2, 4)), -0.2, 0.2), 0.099609375, 1.0).astype(jnp.bfloat16)
    counts = draw_counts(jax.random.fold_in(streams_of[7], 71), 0)
    w_gate = centred(streams_of[4], (N_PIPE, EXPERTS, D // 2, FF), D ** -0.5, 0.125, ((0, 4), (1, 4), (3, 2)))
    w_up = centred(streams_of[5], (N_PIPE, EXPERTS, D // 2, FF), D ** -0.5, 0.125, ((0, 4), (1, 4), (3, 2)))
    w_down = centred(streams_of[6], (N_PIPE, EXPERTS, FF, D // 2), FF ** -0.5, 0.25, ((0, 4), (1, 4), (2, 2)))
    return {"acts": acts, "out_grad": out_grad, "probs": probs, "counts": counts, "w_gate": w_gate, "w_up": w_up, "w_down": w_down}


def silu_parts(gate):
    sigma = jax.nn.sigmoid(gate)
    return gate * sigma, sigma * (1.0 + gate * (1.0 - sigma))


def section_terms(section, acts, out_grad, probs, counts, w_gate, w_up, w_down):
    layers = w_gate.shape[0] // 2
    experts = counts.shape[-1]
    rows = acts.shape[2] // experts
    width = acts.shape[3]
    layer = section % layers
    count_rows = counts[section].astype(jnp.int32)
    ends = jnp.cumsum(count_rows, axis=-1).astype(jnp.int32)
    starts = (ends - count_rows).astype(jnp.int32)
    position = jnp.arange(CAP).astype(jnp.int32)
    live = position < count_rows[..., None]
    local = jnp.where(live, starts[..., None] + position, 0).astype(jnp.int32)
    dir_ids = jnp.arange(2).astype(jnp.int32)[:, None, None, None]
    src_ids = jnp.arange(experts).astype(jnp.int32)[None, :, None, None]
    global_rows = ((dir_ids * experts + src_ids) * rows + local).reshape(-1)
    live_flat = live.reshape(-1)

    def pack_rows(values):
        taken = jnp.take(values.reshape(-1, width), global_rows, axis=0)
        taken = jnp.where(live_flat[:, None], taken, jnp.zeros_like(taken))
        taken = taken.reshape(2, experts, experts, CAP, width)
        return jnp.transpose(taken, (2, 0, 1, 3, 4)).reshape(experts, -1, width)

    slots_x = pack_rows(acts[section])
    slots_g = pack_rows(out_grad[section])
    taken = jnp.take(probs[section].reshape(-1), global_rows, axis=0)
    taken = jnp.where(live_flat, taken, jnp.zeros_like(taken)).reshape(2, experts, experts, CAP)
    slots_p = jnp.transpose(taken, (2, 0, 1, 3)).reshape(experts, -1)

    full_gate = jnp.concatenate([w_gate[layer], w_gate[layer + layers]], axis=1).astype(jnp.float32)
    full_up = jnp.concatenate([w_up[layer], w_up[layer + layers]], axis=1).astype(jnp.float32)
    full_down = jnp.concatenate([w_down[layer], w_down[layer + layers]], axis=2).astype(jnp.float32)

    input_float = slots_x.astype(jnp.float32)
    grad_float = slots_g.astype(jnp.float32)
    gate = jnp.einsum('emd,edf->emf', input_float, full_gate)
    up = jnp.einsum('emd,edf->emf', input_float, full_up)
    silu_value, slope = silu_parts(gate)
    act = (silu_value * up).astype(jnp.bfloat16)
    back = jnp.einsum('emd,efd->emf', grad_float, full_down)
    prob_term = jnp.sum(act.astype(jnp.float32) * back, axis=-1)
    scale = slots_p.astype(jnp.float32)[..., None]
    d_gate = (scale * back * up * slope).astype(jnp.bfloat16)
    d_up = (scale * back * silu_value).astype(jnp.bfloat16)
    scaled = (scale * grad_float).astype(jnp.bfloat16)
    slot_grad = jnp.einsum('emf,edf->emd', d_gate.astype(jnp.float32), full_gate)
    slot_grad = slot_grad + jnp.einsum('emf,edf->emd', d_up.astype(jnp.float32), full_up)
    slot_grad = slot_grad.astype(jnp.bfloat16)
    prob_slot = prob_term.astype(jnp.bfloat16)
    section_gate = jnp.einsum('emd,emf->edf', input_float, d_gate.astype(jnp.float32)).astype(jnp.bfloat16)
    section_up = jnp.einsum('emd,emf->edf', input_float, d_up.astype(jnp.float32)).astype(jnp.bfloat16)
    section_down = jnp.einsum('emf,emd->efd', act.astype(jnp.float32), scaled.astype(jnp.float32)).astype(jnp.bfloat16)

    row_ids = jnp.arange(rows).astype(jnp.int32)
    owner = jnp.sum((ends[:, :, None, :] <= row_ids[None, None, :, None]).astype(jnp.int32), axis=-1).astype(jnp.int32)
    start_row = jnp.take_along_axis(starts, owner, axis=2).astype(jnp.int32)
    dir_two = jnp.arange(2).astype(jnp.int32)[:, None, None]
    src_two = jnp.arange(experts).astype(jnp.int32)[None, :, None]
    slot_place = (((dir_two * experts + src_two) * experts + owner) * CAP + row_ids - start_row).reshape(-1)
    grid = jnp.transpose(slot_grad.reshape(experts, 2, experts, CAP, width), (1, 2, 0, 3, 4)).reshape(-1, width)
    row_grad = jnp.take(grid, slot_place, axis=0).reshape(2, experts * rows, width)
    prob_grid = jnp.transpose(prob_slot.reshape(experts, 2, experts, CAP), (1, 2, 0, 3)).reshape(-1)
    row_prob = jnp.take(prob_grid, slot_place, axis=0).reshape(2, experts * rows)
    return row_grad, row_prob, section_gate, section_up, section_down


def combine(first, second, axis):
    total = (first.astype(jnp.float32) + second.astype(jnp.float32)).astype(jnp.bfloat16)
    half = total.shape[axis] // 2
    lower = lax.slice_in_dim(total, 0, half, axis=axis)
    higher = lax.slice_in_dim(total, half, 2 * half, axis=axis)
    return jnp.stack([lower, higher])


def reference(acts, out_grad, probs, counts, w_gate, w_up, w_down):
    layers = w_gate.shape[0] // 2

    def one_layer(layer):
        lower = section_terms(layer, acts, out_grad, probs, counts, w_gate, w_up, w_down)
        higher = section_terms(layer + layers, acts, out_grad, probs, counts, w_gate, w_up, w_down)
        row_grad = jnp.stack([lower[0], higher[0]])
        row_prob = jnp.stack([lower[1], higher[1]])
        return (row_grad, row_prob, combine(lower[2], higher[2], 1),
                combine(lower[3], higher[3], 1), combine(lower[4], higher[4], 2))

    results = lax.map(one_layer, jnp.arange(layers).astype(jnp.int32))

    def arrange(stacked):
        moved = jnp.swapaxes(stacked, 0, 1)
        return moved.reshape((2 * layers,) + stacked.shape[2:])

    return (arrange(results[0]), arrange(results[1]), arrange(results[2]),
            arrange(results[3]), arrange(results[4]))
```

```python
import functools

import jax
import jax.numpy as jnp
from jax import lax
from jax.experimental import pallas as pl
from jax.experimental.pallas import tpu as pltpu
from jax.sharding import PartitionSpec as P

F32, BF16 = jnp.float32, jnp.bfloat16
MESH = pl.DeviceIdType.MESH


def mm(a, b, dims):
    return lax.dot_general(a, b, (dims, ((), ())), preferred_element_type=F32)


NN, NT, TN = ((1,), (0,)), ((1,), (1,)), ((0,), (0,))


def as_row(column):
    size = column.shape[0]
    eye = lax.broadcasted_iota(jnp.int32, (size, size), 0) == lax.broadcasted_iota(
        jnp.int32, (size, size), 1
    )
    return jnp.sum(jnp.where(eye, column, 0.0), axis=0, keepdims=True)


def as_column(row):
    size = row.shape[1]
    eye = lax.broadcasted_iota(jnp.int32, (size, size), 0) == lax.broadcasted_iota(
        jnp.int32, (size, size), 1
    )
    return jnp.sum(jnp.where(eye, row, 0.0), axis=1, keepdims=True)


def kernel(
    n,
    pipes,
    acts,
    grads,
    probs,
    counts,
    w_gate,
    w_up,
    w_down,
    act_out,
    prob_out,
    gate_out,
    up_out,
    down_out,
    pick,
    pack_x,
    pack_g,
    pack_p,
    xs,
    gs,
    ps,
    wg,
    wu,
    wd,
    dg,
    du,
    ac,
    sc,
    po,
    p_send,
    p_recv,
    q_send,
    q_recv,
    r_send,
    rq_send,
    ret,
    rq,
    dw_send,
    dd_send,
    dw_recv,
    dd_recv,
    send_z,
    recv_z,
    send_x,
    recv_x,
    send_y,
    recv_y,
    send_b,
    recv_b,
    local,
):
    me = lax.axis_index("expert")
    t = lax.axis_index("tensor")
    pipe = lax.axis_index("pipe")
    h = pipe // (pipes // 2)
    over_x = {"tensor": 1 - t}
    over_y = {"pipe": lax.rem(pipe + pipes // 2, pipes)}
    rows = acts.shape[1]
    slots = 2 * rows // n
    block = 2 * slots

    barrier = pltpu.get_barrier_semaphore()
    pl.semaphore_signal(barrier, inc=1, device_id=over_x, device_id_type=MESH)
    pl.semaphore_signal(barrier, inc=1, device_id=over_y, device_id_type=MESH)
    for k in range(1, n):
        pl.semaphore_signal(
            barrier, inc=1, device_id={"expert": lax.rem(me + k, n)}, device_id_type=MESH
        )

    own = [
        pltpu.make_async_copy(src, dst.at[h], local.at[i])
        for i, (src, dst) in enumerate(((w_gate, wg), (w_up, wu), (w_down, wd)))
    ]
    for copy in own:
        copy.start()
    pl.semaphore_wait(barrier, n + 1)
    weights = [
        pltpu.make_async_remote_copy(
            src, dst.at[h], send_y.at[i], recv_y.at[i], device_id=over_y, device_id_type=MESH
        )
        for i, (src, dst) in enumerate(((w_gate, wg), (w_up, wu), (w_down, wd)))
    ]
    for copy in weights:
        copy.start()

    def remote(src, dst, send, recv, where):
        return pltpu.make_async_remote_copy(
            src, dst, send, recv, device_id=where, device_id_type=MESH
        )

    all_x = acts[...].reshape(2 * rows, acts.shape[2])
    all_g = grads[...].reshape(2 * rows, grads.shape[2])
    all_p = jnp.concatenate([probs[0:1, :].astype(F32), probs[1:2, :].astype(F32)], axis=1)
    all_p = jnp.broadcast_to(all_p, (16, 2 * rows)).astype(BF16)
    slot = lax.broadcasted_iota(jnp.int32, (slots, 2 * rows), 0)
    lane = lax.broadcasted_iota(jnp.int32, (slots, 2 * rows), 1)
    starts = [jnp.int32(0), jnp.int32(0)]
    for e in range(n):
        for d in range(2):
            count = counts[d, e]
            hit = (lane == slot + (starts[d] + d * rows)) & (slot < count)
            pick[e, d * slots : (d + 1) * slots, :] = jnp.where(hit, 1.0, 0.0).astype(BF16)
            starts[d] = starts[d] + count

    def forward(s, which):
        buf = (xs, gs)[which]
        return remote(
            buf.at[t, s], buf.at[t, s], send_x.at[which, s], recv_x.at[which, s], over_x
        )

    def backward(s, which):
        src, dst = ((p_send, p_recv), (q_send, q_recv))[which]
        return remote(
            src.at[s], dst.at[s], send_x.at[2 + which, s], recv_x.at[2 + which, s], over_x
        )

    def to_expert(e, which):
        src, dst = (
            (pack_x.at[e], xs.at[t, me]),
            (pack_g.at[e], gs.at[t, me]),
            (pack_p.at[e], ps.at[me]),
        )[which]
        return remote(src, dst, send_z.at[which, e], recv_z.at[which, me], {"expert": e})

    def from_source(s, which):
        dst = (xs.at[t, s], gs.at[t, s], ps.at[s])[which]
        return remote(dst, dst, send_z.at[which, s], recv_z.at[which, s], {"expert": s})

    def to_source(s, which):
        src, dst = ((r_send.at[s], ret.at[me]), (rq_send.at[s], rq.at[me]))[which]
        return remote(src, dst, send_z.at[3 + which, s], recv_z.at[3 + which, me], {"expert": s})

    def from_expert(e, which):
        dst = (ret.at[e], rq.at[e])[which]
        return remote(dst, dst, send_z.at[3 + which, e], recv_z.at[3 + which, e], {"expert": e})

    order = [lax.rem(me + k, n) for k in range(n)]
    came = [lax.rem(me + n - k, n) for k in range(n)]
    xs[t, me] = mm(pick[me], all_x, NN).astype(BF16)
    forward(me, 0).start()
    for e in order[1:]:
        pack_x[e] = mm(pick[e], all_x, NN).astype(BF16)
        to_expert(e, 0).start()
    gs[t, me] = mm(pick[me], all_g, NN).astype(BF16)
    ps[me] = mm(all_p, pick[me], NT).astype(BF16)
    forward(me, 1).start()
    for e in order[1:]:
        pack_g[e] = mm(pick[e], all_g, NN).astype(BF16)
        to_expert(e, 1).start()
        pack_p[e] = mm(all_p, pick[e], NT).astype(BF16)
        to_expert(e, 2).start()

    for which in range(2):
        for s in came[1:]:
            from_source(s, which).wait_recv()
            forward(s, which).start()

    for copy in own:
        copy.wait()

    def settle_rows(s):
        backward(s, 0).wait_recv()
        backward(s, 1).wait_recv()
        total = po[s] + p_recv[s].astype(F32)
        prob = jnp.broadcast_to((q_send[s] + q_recv[s])[0:1], (16, block))
        return total.astype(BF16), prob.astype(BF16)

    def return_rows(s):
        total, prob = settle_rows(s)
        r_send[s] = total
        rq_send[s] = prob
        to_source(s, 0).start()
        to_source(s, 1).start()

    for at, s in enumerate(came):
        if at == 0:
            for copy in weights:
                copy.wait_recv()
        else:
            from_source(s, 2).wait_recv()
        other = (xs.at[1 - t, s], gs.at[1 - t, s])
        for which in range(2):
            remote(
                other[which], other[which], send_x.at[which, s], recv_x.at[which, s], over_x
            ).wait_recv()
        gate = mm(xs[0, s], wg[0], NN) + mm(xs[1, s], wg[1], NN)
        up = mm(xs[0, s], wu[0], NN) + mm(xs[1, s], wu[1], NN)
        back = mm(gs[0, s], wd[0], NT) + mm(gs[1, s], wd[1], NT)
        sigma = jax.nn.sigmoid(gate)
        silu = gate * sigma
        act = (silu * up).astype(BF16)
        ac[s] = act
        prob_term = jnp.sum(act.astype(F32) * back, axis=1, keepdims=True)
        scale = as_column(ps[s].astype(F32)[0:1])
        scaled = scale * back
        d_gate = (scaled * up * (sigma * (1.0 + gate * (1.0 - sigma)))).astype(BF16)
        d_up = (scaled * silu).astype(BF16)
        dg[s] = d_gate
        du[s] = d_up
        p_send[s] = (mm(d_gate, wg[1 - t], NT) + mm(d_up, wu[1 - t], NT)).astype(BF16)
        q_send[s] = jnp.broadcast_to(as_row(prob_term), (8, block))
        backward(s, 0).start()
        backward(s, 1).start()
        po[s] = mm(d_gate, wg[t], NT) + mm(d_up, wu[t], NT)
        sc[0, s] = (scale * gs[0, s].astype(F32)).astype(BF16)
        sc[1, s] = (scale * gs[1, s].astype(F32)).astype(BF16)
        if at >= 2:
            return_rows(came[at - 1])

    def terms(half, i):
        depth = n * block
        if i == 2:
            return mm(
                ac[...].reshape(depth, ac.shape[2]), sc[half].reshape(depth, sc.shape[3]), TN
            )
        d = (dg, du)[i]
        return mm(xs[half].reshape(depth, xs.shape[3]), d[...].reshape(depth, d.shape[2]), TN)

    partials = [
        remote(src, dst, send_b.at[i], recv_b.at[i], over_y)
        for i, (src, dst) in enumerate(
            (
                (dw_send.at[0], dw_recv.at[0]),
                (dw_send.at[1], dw_recv.at[1]),
                (dd_send, dd_recv),
            )
        )
    ]
    for i in range(2):
        dw_send[i] = terms(1 - h, i).astype(BF16)
        partials[i].start()
    dd_send[...] = terms(1 - h, 2).astype(BF16)
    partials[2].start()

    if n > 1:
        return_rows(came[n - 1])
    total, prob = settle_rows(me)
    ret[me] = total
    rq[me] = prob
    keep = [terms(h, i) for i in range(3)]
    partials[0].wait_recv()
    gate_out[...] = (keep[0] + dw_recv[0].astype(F32)).astype(BF16)

    for e in order[1:]:
        from_expert(e, 0).wait_recv()
        from_expert(e, 1).wait_recv()
    chosen = pick[...].reshape(n * block, 2 * rows)
    back_rows = mm(chosen, ret[...].reshape(n * block, ret.shape[2]), TN)
    act_out[...] = back_rows.astype(BF16).reshape(act_out.shape)
    back_prob = jnp.zeros((16, 2 * rows), F32)
    for e in range(n):
        back_prob = back_prob + mm(rq[e], pick[e], NN)
    prob_out[0:1, :] = back_prob[0:1, :rows].astype(BF16)
    prob_out[1:2, :] = back_prob[0:1, rows:].astype(BF16)

    partials[1].wait_recv()
    up_out[...] = (keep[1] + dw_recv[1].astype(F32)).astype(BF16)
    partials[2].wait_recv()
    down_out[...] = (keep[2] + dd_recv[...].astype(F32)).astype(BF16)

    for copy in weights + partials:
        copy.wait_send()
    for s in came:
        for which in range(2):
            forward(s, which).wait_send()
            backward(s, which).wait_send()
    for e in order[1:]:
        for which in range(3):
            to_expert(e, which).wait_send()
        for which in range(2):
            to_source(e, which).wait_send()


def on_device(acts, out_grad, probs, counts, w_gate, w_up, w_down):
    n = lax.axis_size("expert")
    pipes = lax.axis_size("pipe")
    rows, width = acts.shape[2], acts.shape[3]
    slots = 2 * rows // n
    block = 2 * slots
    deep, hidden = w_gate.shape[2], w_gate.shape[3]
    v = pltpu.VMEM
    dma = pltpu.SemaphoreType.DMA
    vmem = pl.BlockSpec(memory_space=pltpu.VMEM)
    hbm = pl.BlockSpec(memory_space=pl.ANY)
    outs = pl.pallas_call(
        functools.partial(kernel, n, pipes),
        out_shape=(
            jax.ShapeDtypeStruct((2, rows, width), BF16),
            jax.ShapeDtypeStruct((2, rows), BF16),
            jax.ShapeDtypeStruct((deep, hidden), BF16),
            jax.ShapeDtypeStruct((deep, hidden), BF16),
            jax.ShapeDtypeStruct((hidden, deep), BF16),
        ),
        in_specs=[vmem, vmem, vmem, pl.BlockSpec(memory_space=pltpu.SMEM), hbm, hbm, hbm],
        out_specs=(vmem,) * 5,
        scratch_shapes=[
            v((n, block, 2 * rows), BF16),
            v((n, block, width), BF16),
            v((n, block, width), BF16),
            v((n, 16, block), BF16),
            v((2, n, block, width), BF16),
            v((2, n, block, width), BF16),
            v((n, 16, block), BF16),
            v((2, deep, hidden), BF16),
            v((2, deep, hidden), BF16),
            v((2, hidden, deep), BF16),
            v((n, block, hidden), BF16),
            v((n, block, hidden), BF16),
            v((n, block, hidden), BF16),
            v((2, n, block, width), BF16),
            v((n, block, width), F32),
            v((n, block, width), BF16),
            v((n, block, width), BF16),
            v((n, 8, block), F32),
            v((n, 8, block), F32),
            v((n, block, width), BF16),
            v((n, 16, block), BF16),
            v((n, block, width), BF16),
            v((n, 16, block), BF16),
            v((2, deep, hidden), BF16),
            v((hidden, deep), BF16),
            v((2, deep, hidden), BF16),
            v((hidden, deep), BF16),
            dma((5, n)),
            dma((5, n)),
            dma((4, n)),
            dma((4, n)),
            dma((3,)),
            dma((3,)),
            dma((3,)),
            dma((3,)),
            dma((3,)),
        ],
        compiler_params=pltpu.CompilerParams(
            collective_id=0, has_side_effects=True, vmem_limit_bytes=56 << 20
        ),
    )(acts[0], out_grad[0], probs[0], counts[0, :, 0, :], w_gate[0, 0], w_up[0, 0], w_down[0, 0])
    return (outs[0][None], outs[1][None]) + tuple(o[None, None] for o in outs[2:])


def solution(mesh):
    return jax.shard_map(
        on_device,
        mesh=mesh,
        in_specs=(
            P("pipe", None, "expert", "tensor"),
            P("pipe", None, "expert", "tensor"),
            P("pipe", None, "expert"),
            P("pipe", None, "expert", None),
            P("pipe", "expert", None, "tensor"),
            P("pipe", "expert", None, "tensor"),
            P("pipe", "expert", "tensor", None),
        ),
        out_specs=(
            P("pipe", None, "expert", "tensor"),
            P("pipe", None, "expert"),
            P("pipe", "expert", None, "tensor"),
            P("pipe", "expert", None, "tensor"),
            P("pipe", "expert", "tensor", None),
        ),
        check_vma=False,
    )
```

```python
import functools

import jax
import jax.numpy as jnp
from jax import lax
from jax.experimental import pallas as pl
from jax.experimental.pallas import tpu as pltpu
from jax.sharding import PartitionSpec as P

F32, BF16 = jnp.float32, jnp.bfloat16
MESH = pl.DeviceIdType.MESH


def mm(a, b, dims):
    return lax.dot_general(a, b, (dims, ((), ())), preferred_element_type=F32)


NN, NT, TN = ((1,), (0,)), ((1,), (1,)), ((0,), (0,))


def as_row(column):
    size = column.shape[0]
    eye = lax.broadcasted_iota(jnp.int32, (size, size), 0) == lax.broadcasted_iota(
        jnp.int32, (size, size), 1
    )
    return jnp.sum(jnp.where(eye, column, 0.0), axis=0, keepdims=True)


def as_column(row):
    size = row.shape[1]
    eye = lax.broadcasted_iota(jnp.int32, (size, size), 0) == lax.broadcasted_iota(
        jnp.int32, (size, size), 1
    )
    return jnp.sum(jnp.where(eye, row, 0.0), axis=1, keepdims=True)


def kernel(
    n,
    pipes,
    acts,
    grads,
    probs,
    counts,
    w_gate,
    w_up,
    w_down,
    act_out,
    prob_out,
    gate_out,
    up_out,
    down_out,
    pick,
    pack_x,
    pack_g,
    pack_p,
    xs,
    gs,
    ps,
    wg,
    wu,
    wd,
    dg,
    du,
    ac,
    silus,
    slopes,
    acts_f,
    sums,
    sum_d,
    po,
    p_send,
    p_recv,
    q_send,
    q_recv,
    r_send,
    rq_send,
    ret,
    rq,
    dw_send,
    dd_send,
    dw_recv,
    dd_recv,
    send_z,
    recv_z,
    send_x,
    recv_x,
    send_p,
    recv_p,
    send_y,
    recv_y,
    send_b,
    recv_b,
    local,
):
    me = lax.axis_index("expert")
    t = lax.axis_index("tensor")
    pipe = lax.axis_index("pipe")
    h = pipe // (pipes // 2)
    over_x = {"tensor": 1 - t}
    over_y = {"pipe": lax.rem(pipe + pipes // 2, pipes)}
    rows = acts.shape[1]
    slots = 2 * rows // n
    block = 2 * slots

    barrier = pltpu.get_barrier_semaphore()
    pl.semaphore_signal(barrier, inc=1, device_id=over_x, device_id_type=MESH)
    pl.semaphore_signal(barrier, inc=1, device_id=over_y, device_id_type=MESH)
    for k in range(1, n):
        pl.semaphore_signal(
            barrier, inc=1, device_id={"expert": lax.rem(me + k, n)}, device_id_type=MESH
        )

    own = [
        pltpu.make_async_copy(src, dst.at[h], local.at[i])
        for i, (src, dst) in enumerate(((w_gate, wg), (w_up, wu), (w_down, wd)))
    ]
    for copy in own:
        copy.start()
    pl.semaphore_wait(barrier, n + 1)
    weights = [
        pltpu.make_async_remote_copy(
            src, dst.at[h], send_y.at[i], recv_y.at[i], device_id=over_y, device_id_type=MESH
        )
        for i, (src, dst) in enumerate(((w_gate, wg), (w_up, wu), (w_down, wd)))
    ]
    for copy in weights:
        copy.start()

    def remote(src, dst, send, recv, where):
        return pltpu.make_async_remote_copy(
            src, dst, send, recv, device_id=where, device_id_type=MESH
        )

    all_x = acts[...].reshape(2 * rows, acts.shape[2])
    all_g = grads[...].reshape(2 * rows, grads.shape[2])
    all_p = jnp.concatenate([probs[0:1, :].astype(F32), probs[1:2, :].astype(F32)], axis=1)
    all_p = jnp.broadcast_to(all_p, (16, 2 * rows)).astype(BF16)
    slot = lax.broadcasted_iota(jnp.int32, (slots, 2 * rows), 0)
    lane = lax.broadcasted_iota(jnp.int32, (slots, 2 * rows), 1)
    starts = [jnp.int32(0), jnp.int32(0)]
    for e in range(n):
        for d in range(2):
            count = counts[d, e]
            hit = (lane == slot + (starts[d] + d * rows)) & (slot < count)
            pick[e, d * slots : (d + 1) * slots, :] = jnp.where(hit, 1.0, 0.0).astype(BF16)
            starts[d] = starts[d] + count

    def part(which):
        return pl.ds(which % 2 * slots, slots)

    def forward(s, which, half):
        at = (xs, gs)[which // 2].at[half, s, part(which)]
        return remote(at, at, send_x.at[which, s], recv_x.at[which, s], over_x)

    def backward(s, which):
        src, dst = ((p_send, p_recv), (q_send, q_recv))[which]
        return remote(src.at[s], dst.at[s], send_p.at[which, s], recv_p.at[which, s], over_x)

    def to_expert(e, which):
        if which == 4:
            src, dst = pack_p.at[e], ps.at[me]
        else:
            pack, buf = ((pack_x, xs), (pack_g, gs))[which // 2]
            src, dst = pack.at[e, part(which)], buf.at[t, me, part(which)]
        return remote(src, dst, send_z.at[which, e], recv_z.at[which, me], {"expert": e})

    def from_source(s, which):
        dst = ps.at[s] if which == 4 else (xs, gs)[which // 2].at[t, s, part(which)]
        return remote(dst, dst, send_z.at[which, s], recv_z.at[which, s], {"expert": s})

    def to_source(s, which):
        src, dst = ((r_send.at[s], ret.at[me]), (rq_send.at[s], rq.at[me]))[which]
        return remote(src, dst, send_z.at[5 + which, s], recv_z.at[5 + which, me], {"expert": s})

    def from_expert(e, which):
        dst = (ret.at[e], rq.at[e])[which]
        return remote(dst, dst, send_z.at[5 + which, e], recv_z.at[5 + which, e], {"expert": e})

    order = [lax.rem(me + k, n) for k in range(n)]
    came = [lax.rem(me + n - k, n) for k in range(n)]
    xs[t, me] = mm(pick[me], all_x, NN).astype(BF16)
    for which in (0, 1):
        forward(me, which, t).start()
    for e in order[1:]:
        pack_x[e] = mm(pick[e], all_x, NN).astype(BF16)
        for which in (0, 1):
            to_expert(e, which).start()
    gs[t, me] = mm(pick[me], all_g, NN).astype(BF16)
    ps[me] = mm(all_p, pick[me], NT).astype(BF16)
    for which in (2, 3):
        forward(me, which, t).start()
    for e in order[1:]:
        pack_g[e] = mm(pick[e], all_g, NN).astype(BF16)
        pack_p[e] = mm(all_p, pick[e], NT).astype(BF16)
        for which in (2, 3, 4):
            to_expert(e, which).start()

    for whiches in ((0, 1), (2, 3)):
        for s in came[1:]:
            for which in whiches:
                from_source(s, which).wait_recv()
                forward(s, which, t).start()

    for copy in own:
        copy.wait()

    def settle_rows(s):
        backward(s, 0).wait_recv()
        backward(s, 1).wait_recv()
        total = po[s] + p_recv[s].astype(F32)
        prob = jnp.broadcast_to((q_send[s] + q_recv[s])[0:1], (16, block))
        return total.astype(BF16), prob.astype(BF16)

    def return_rows(s):
        total, prob = settle_rows(s)
        r_send[s] = total
        rq_send[s] = prob
        to_source(s, 0).start()
        to_source(s, 1).start()

    for copy in weights:
        copy.wait_recv()
    for s in came:
        for which in (0, 1):
            forward(s, which, 1 - t).wait_recv()
        gate = mm(xs[0, s], wg[0], NN) + mm(xs[1, s], wg[1], NN)
        up = mm(xs[0, s], wu[0], NN) + mm(xs[1, s], wu[1], NN)
        sigma = jax.nn.sigmoid(gate)
        silu = gate * sigma
        silus[s] = silu
        slopes[s] = up * (sigma * (1.0 + gate * (1.0 - sigma)))
        acts_f[s] = silu * up

    def send_rows(s):
        p_send[s] = (mm(dg[s], wg[1 - t], NT) + mm(du[s], wu[1 - t], NT)).astype(BF16)
        backward(s, 0).start()
        backward(s, 1).start()
        po[s] = mm(dg[s], wg[t], NT) + mm(du[s], wu[t], NT)

    def joined(ref, which):
        return jnp.concatenate([ref[s] for s in which], axis=0)

    def terms(half, i, which):
        if i == 2:
            return mm(joined(ac, which), joined(gs.at[half], which), TN)
        return mm(joined(xs.at[half], which), joined((dg, du)[i], which), TN)

    def later_rows(at):
        send_rows(came[at])
        if at >= 2:
            return_rows(came[at - 1])

    for at, s in enumerate(came):
        if at > 0:
            from_source(s, 4).wait_recv()
        for which in (2, 3):
            forward(s, which, 1 - t).wait_recv()
        back = mm(gs[0, s], wd[0], NT) + mm(gs[1, s], wd[1], NT)
        act = acts_f[s]
        prob_term = jnp.sum(act.astype(BF16).astype(F32) * back, axis=1, keepdims=True)
        q_send[s] = jnp.broadcast_to(as_row(prob_term), (8, block))
        scale = as_column(ps[s].astype(F32)[0:1])
        ac[s] = (scale * act).astype(BF16)
        scaled = scale * back
        dg[s] = (scaled * slopes[s]).astype(BF16)
        du[s] = (scaled * silus[s]).astype(BF16)
        if at < n - 1:
            later_rows(at)
        if at == n - 2:
            for i in range(2):
                sums[i] = terms(1 - h, i, came[: n - 1])
            sum_d[...] = terms(1 - h, 2, came[: n - 1])

    partials = [
        remote(src, dst, send_b.at[i], recv_b.at[i], over_y)
        for i, (src, dst) in enumerate(
            (
                (dw_send.at[0], dw_recv.at[0]),
                (dw_send.at[1], dw_recv.at[1]),
                (dd_send, dd_recv),
            )
        )
    ]
    last = came[n - 1 :]
    for i in range(2):
        dw_send[i] = (sums[i] + terms(1 - h, i, last)).astype(BF16)
        partials[i].start()
    dd_send[...] = (sum_d[...] + terms(1 - h, 2, last)).astype(BF16)
    partials[2].start()
    later_rows(n - 1)

    return_rows(came[n - 1])
    total, prob = settle_rows(me)
    ret[me] = total
    rq[me] = prob
    keep = [terms(h, i, range(n)) for i in range(3)]
    partials[0].wait_recv()
    gate_out[...] = (keep[0] + dw_recv[0].astype(F32)).astype(BF16)

    for e in order[1:]:
        from_expert(e, 0).wait_recv()
        from_expert(e, 1).wait_recv()
    chosen = pick[...].reshape(n * block, 2 * rows)
    back_rows = mm(chosen, ret[...].reshape(n * block, ret.shape[2]), TN)
    act_out[...] = back_rows.astype(BF16).reshape(act_out.shape)
    back_prob = jnp.zeros((16, 2 * rows), F32)
    for e in range(n):
        back_prob = back_prob + mm(rq[e], pick[e], NN)
    prob_out[0:1, :] = back_prob[0:1, :rows].astype(BF16)
    prob_out[1:2, :] = back_prob[0:1, rows:].astype(BF16)

    partials[1].wait_recv()
    up_out[...] = (keep[1] + dw_recv[1].astype(F32)).astype(BF16)
    partials[2].wait_recv()
    down_out[...] = (keep[2] + dd_recv[...].astype(F32)).astype(BF16)

    for copy in weights + partials:
        copy.wait_send()
    for s in came:
        for which in range(4):
            forward(s, which, t).wait_send()
        for which in range(2):
            backward(s, which).wait_send()
    for e in order[1:]:
        for which in range(5):
            to_expert(e, which).wait_send()
        for which in range(2):
            to_source(e, which).wait_send()


def hand_over(*refs):
    copies = [pltpu.make_async_copy(refs[i], refs[5 + i], refs[10].at[i]) for i in range(5)]
    for copy in copies:
        copy.start()
    for copy in copies:
        copy.wait()


def on_device(acts, out_grad, probs, counts, w_gate, w_up, w_down):
    n = lax.axis_size("expert")
    pipes = lax.axis_size("pipe")
    rows, width = acts.shape[2], acts.shape[3]
    slots = 2 * rows // n
    block = 2 * slots
    deep, hidden = w_gate.shape[2], w_gate.shape[3]
    v = pltpu.VMEM
    dma = pltpu.SemaphoreType.DMA
    vmem = pl.BlockSpec(memory_space=pltpu.VMEM)
    hbm = pl.BlockSpec(memory_space=pl.ANY)
    outs = pl.pallas_call(
        functools.partial(kernel, n, pipes),
        out_shape=(
            jax.ShapeDtypeStruct((2, rows, width), BF16),
            jax.ShapeDtypeStruct((2, rows), BF16),
            jax.ShapeDtypeStruct((deep, hidden), BF16),
            jax.ShapeDtypeStruct((deep, hidden), BF16),
            jax.ShapeDtypeStruct((hidden, deep), BF16),
        ),
        in_specs=[vmem, vmem, vmem, pl.BlockSpec(memory_space=pltpu.SMEM), hbm, hbm, hbm],
        out_specs=(vmem,) * 5,
        scratch_shapes=[
            v((n, block, 2 * rows), BF16),
            v((n, block, width), BF16),
            v((n, block, width), BF16),
            v((n, 16, block), BF16),
            v((2, n, block, width), BF16),
            v((2, n, block, width), BF16),
            v((n, 16, block), BF16),
            v((2, deep, hidden), BF16),
            v((2, deep, hidden), BF16),
            v((2, hidden, deep), BF16),
            v((n, block, hidden), BF16),
            v((n, block, hidden), BF16),
            v((n, block, hidden), BF16),
            v((n, block, hidden), F32),
            v((n, block, hidden), F32),
            v((n, block, hidden), F32),
            v((2, deep, hidden), F32),
            v((hidden, deep), F32),
            v((n, block, width), F32),
            v((n, block, width), BF16),
            v((n, block, width), BF16),
            v((n, 8, block), F32),
            v((n, 8, block), F32),
            v((n, block, width), BF16),
            v((n, 16, block), BF16),
            v((n, block, width), BF16),
            v((n, 16, block), BF16),
            v((2, deep, hidden), BF16),
            v((hidden, deep), BF16),
            v((2, deep, hidden), BF16),
            v((hidden, deep), BF16),
            dma((7, n)),
            dma((7, n)),
            dma((4, n)),
            dma((4, n)),
            dma((2, n)),
            dma((2, n)),
            dma((3,)),
            dma((3,)),
            dma((3,)),
            dma((3,)),
            dma((3,)),
        ],
        compiler_params=pltpu.CompilerParams(
            collective_id=0, has_side_effects=True, vmem_limit_bytes=56 << 20
        ),
    )(acts[0], out_grad[0], probs[0], counts[0, :, 0, :], w_gate[0, 0], w_up[0, 0], w_down[0, 0])
    outs = pl.pallas_call(
        hand_over,
        out_shape=[jax.ShapeDtypeStruct(o.shape, o.dtype) for o in outs],
        in_specs=[vmem] * 5,
        out_specs=[hbm] * 5,
        scratch_shapes=[dma((5,))],
    )(*outs)
    return (outs[0][None], outs[1][None]) + tuple(o[None, None] for o in outs[2:])


def solution(mesh):
    return jax.shard_map(
        on_device,
        mesh=mesh,
        in_specs=(
            P("pipe", None, "expert", "tensor"),
            P("pipe", None, "expert", "tensor"),
            P("pipe", None, "expert"),
            P("pipe", None, "expert", None),
            P("pipe", "expert", None, "tensor"),
            P("pipe", "expert", None, "tensor"),
            P("pipe", "expert", "tensor", None),
        ),
        out_specs=(
            P("pipe", None, "expert", "tensor"),
            P("pipe", None, "expert"),
            P("pipe", "expert", None, "tensor"),
            P("pipe", "expert", None, "tensor"),
            P("pipe", "expert", "tensor", None),
        ),
        check_vma=False,
    )
```

```python
import functools

import jax
import jax.numpy as jnp
from jax import lax
from jax.experimental import pallas as pl
from jax.experimental.pallas import tpu as pltpu
from jax.sharding import PartitionSpec as P

F32, BF16 = jnp.float32, jnp.bfloat16
MESH = pl.DeviceIdType.MESH


def mm(a, b, dims):
    return lax.dot_general(a, b, (dims, ((), ())), preferred_element_type=F32)


NN, NT, TN = ((1,), (0,)), ((1,), (1,)), ((0,), (0,))


def as_row(column):
    size = column.shape[0]
    eye = lax.broadcasted_iota(jnp.int32, (size, size), 0) == lax.broadcasted_iota(
        jnp.int32, (size, size), 1
    )
    return jnp.sum(jnp.where(eye, column, 0.0), axis=0, keepdims=True)


def as_column(row):
    size = row.shape[1]
    eye = lax.broadcasted_iota(jnp.int32, (size, size), 0) == lax.broadcasted_iota(
        jnp.int32, (size, size), 1
    )
    return jnp.sum(jnp.where(eye, row, 0.0), axis=1, keepdims=True)


def kernel(
    n,
    pipes,
    acts,
    grads,
    probs,
    counts,
    w_gate,
    w_up,
    w_down,
    act_out,
    prob_out,
    gate_out,
    up_out,
    down_out,
    pick,
    pack_x,
    pack_g,
    pack_p,
    xs,
    gs,
    ps,
    wg,
    wu,
    wd,
    dg,
    du,
    ac,
    silus,
    slopes,
    acts_f,
    sums,
    sum_d,
    po,
    p_send,
    p_recv,
    q_send,
    q_recv,
    r_send,
    rq_send,
    ret,
    rq,
    dw_send,
    dd_send,
    dw_recv,
    dd_recv,
    send_z,
    recv_z,
    send_x,
    recv_x,
    send_p,
    recv_p,
    send_y,
    recv_y,
    send_b,
    recv_b,
    local,
):
    me = lax.axis_index("expert")
    t = lax.axis_index("tensor")
    pipe = lax.axis_index("pipe")
    h = pipe // (pipes // 2)
    over_x = {"tensor": 1 - t}
    over_y = {"pipe": lax.rem(pipe + pipes // 2, pipes)}
    rows = acts.shape[1]
    slots = 2 * rows // n
    block = 2 * slots

    barrier = pltpu.get_barrier_semaphore()
    pl.semaphore_signal(barrier, inc=1, device_id=over_x, device_id_type=MESH)
    pl.semaphore_signal(barrier, inc=1, device_id=over_y, device_id_type=MESH)
    for k in range(1, n):
        pl.semaphore_signal(
            barrier, inc=1, device_id={"expert": lax.rem(me + k, n)}, device_id_type=MESH
        )

    own = [
        pltpu.make_async_copy(src, dst.at[h], local.at[i])
        for i, (src, dst) in enumerate(((w_gate, wg), (w_up, wu), (w_down, wd)))
    ]
    for copy in own:
        copy.start()
    pl.semaphore_wait(barrier, n + 1)
    weights = [
        pltpu.make_async_remote_copy(
            src, dst.at[h], send_y.at[i], recv_y.at[i], device_id=over_y, device_id_type=MESH
        )
        for i, (src, dst) in enumerate(((w_gate, wg), (w_up, wu), (w_down, wd)))
    ]
    for copy in weights:
        copy.start()

    def remote(src, dst, send, recv, where):
        return pltpu.make_async_remote_copy(
            src, dst, send, recv, device_id=where, device_id_type=MESH
        )

    all_x = acts[...].reshape(2 * rows, acts.shape[2])
    all_g = grads[...].reshape(2 * rows, grads.shape[2])
    all_p = jnp.concatenate([probs[0:1, :].astype(F32), probs[1:2, :].astype(F32)], axis=1)
    all_p = jnp.broadcast_to(all_p, (16, 2 * rows)).astype(BF16)
    slot = lax.broadcasted_iota(jnp.int32, (slots, 2 * rows), 0)
    lane = lax.broadcasted_iota(jnp.int32, (slots, 2 * rows), 1)
    starts = [jnp.int32(0), jnp.int32(0)]
    for e in range(n):
        for d in range(2):
            count = counts[d, e]
            hit = (lane == slot + (starts[d] + d * rows)) & (slot < count)
            pick[e, d * slots : (d + 1) * slots, :] = jnp.where(hit, 1.0, 0.0).astype(BF16)
            starts[d] = starts[d] + count

    def part(which):
        return pl.ds(which % 2 * slots, slots)

    def forward(s, which, half):
        at = (xs, gs)[which // 2].at[half, s, part(which)]
        return remote(at, at, send_x.at[which, s], recv_x.at[which, s], over_x)

    def backward(s, which):
        src, dst = ((p_send, p_recv), (q_send, q_recv))[which]
        return remote(src.at[s], dst.at[s], send_p.at[which, s], recv_p.at[which, s], over_x)

    def to_expert(e, which):
        if which == 4:
            src, dst = pack_p.at[e], ps.at[me]
        else:
            pack, buf = ((pack_x, xs), (pack_g, gs))[which // 2]
            src, dst = pack.at[e, part(which)], buf.at[t, me, part(which)]
        return remote(src, dst, send_z.at[which, e], recv_z.at[which, me], {"expert": e})

    def from_source(s, which):
        dst = ps.at[s] if which == 4 else (xs, gs)[which // 2].at[t, s, part(which)]
        return remote(dst, dst, send_z.at[which, s], recv_z.at[which, s], {"expert": s})

    def to_source(s, which):
        src, dst = ((r_send.at[s], ret.at[me]), (rq_send.at[s], rq.at[me]))[which]
        return remote(src, dst, send_z.at[5 + which, s], recv_z.at[5 + which, me], {"expert": s})

    def from_expert(e, which):
        dst = (ret.at[e], rq.at[e])[which]
        return remote(dst, dst, send_z.at[5 + which, e], recv_z.at[5 + which, e], {"expert": e})

    turns = [0] + sorted(range(1, n), key=lambda k: -abs(2 * k - n))
    order = [lax.rem(me + k, n) for k in turns]
    came = [lax.rem(me + n - k, n) for k in turns]
    xs[t, me] = mm(pick[me], all_x, NN).astype(BF16)
    for which in (0, 1):
        forward(me, which, t).start()
    for e in order[1:]:
        pack_x[e] = mm(pick[e], all_x, NN).astype(BF16)
        for which in (0, 1):
            to_expert(e, which).start()
    gs[t, me] = mm(pick[me], all_g, NN).astype(BF16)
    ps[me] = mm(all_p, pick[me], NT).astype(BF16)
    for which in (2, 3):
        forward(me, which, t).start()
    for e in order[1:]:
        pack_g[e] = mm(pick[e], all_g, NN).astype(BF16)
        pack_p[e] = mm(all_p, pick[e], NT).astype(BF16)
        for which in (2, 3, 4):
            to_expert(e, which).start()

    for whiches in ((0, 1), (2, 3)):
        for s in came[1:]:
            for which in whiches:
                from_source(s, which).wait_recv()
                forward(s, which, t).start()

    for copy in own:
        copy.wait()

    def settle_rows(s):
        backward(s, 0).wait_recv()
        backward(s, 1).wait_recv()
        total = po[s] + p_recv[s].astype(F32)
        prob = jnp.broadcast_to((q_send[s] + q_recv[s])[0:1], (16, block))
        return total.astype(BF16), prob.astype(BF16)

    def return_rows(s):
        total, prob = settle_rows(s)
        r_send[s] = total
        rq_send[s] = prob
        to_source(s, 0).start()
        to_source(s, 1).start()

    for copy in weights:
        copy.wait_recv()
    for s in came:
        for which in (0, 1):
            forward(s, which, 1 - t).wait_recv()
        gate = mm(xs[0, s], wg[0], NN) + mm(xs[1, s], wg[1], NN)
        up = mm(xs[0, s], wu[0], NN) + mm(xs[1, s], wu[1], NN)
        sigma = jax.nn.sigmoid(gate)
        silu = gate * sigma
        silus[s] = silu
        slopes[s] = up * (sigma * (1.0 + gate * (1.0 - sigma)))
        acts_f[s] = silu * up

    def send_rows(s):
        p_send[s] = (mm(dg[s], wg[1 - t], NT) + mm(du[s], wu[1 - t], NT)).astype(BF16)
        backward(s, 0).start()
        backward(s, 1).start()
        po[s] = mm(dg[s], wg[t], NT) + mm(du[s], wu[t], NT)

    def joined(ref, which):
        return jnp.concatenate([ref[s] for s in which], axis=0)

    def terms(half, i, which):
        if i == 2:
            return mm(joined(ac, which), joined(gs.at[half], which), TN)
        return mm(joined(xs.at[half], which), joined((dg, du)[i], which), TN)

    for at, s in enumerate(came):
        if at > 0:
            from_source(s, 4).wait_recv()
        for which in (2, 3):
            forward(s, which, 1 - t).wait_recv()
        back = mm(gs[0, s], wd[0], NT) + mm(gs[1, s], wd[1], NT)
        act = acts_f[s]
        prob_term = jnp.sum(act.astype(BF16).astype(F32) * back, axis=1, keepdims=True)
        q_send[s] = jnp.broadcast_to(as_row(prob_term), (8, block))
        scale = as_column(ps[s].astype(F32)[0:1])
        ac[s] = (scale * act).astype(BF16)
        scaled = scale * back
        dg[s] = (scaled * slopes[s]).astype(BF16)
        du[s] = (scaled * silus[s]).astype(BF16)
        if at < n - 1:
            send_rows(s)
        if at == n - 2:
            for i in range(2):
                sums[i] = terms(1 - h, i, came[: n - 1])
            sum_d[...] = terms(1 - h, 2, came[: n - 1])

    partials = [
        remote(src, dst, send_b.at[i], recv_b.at[i], over_y)
        for i, (src, dst) in enumerate(
            (
                (dw_send.at[0], dw_recv.at[0]),
                (dw_send.at[1], dw_recv.at[1]),
                (dd_send, dd_recv),
            )
        )
    ]
    last = came[n - 1 :]
    for i in range(2):
        dw_send[i] = (sums[i] + terms(1 - h, i, last)).astype(BF16)
        partials[i].start()
    dd_send[...] = (sum_d[...] + terms(1 - h, 2, last)).astype(BF16)
    partials[2].start()
    send_rows(came[n - 1])

    for s in came[1:]:
        return_rows(s)
    total, prob = settle_rows(me)
    ret[me] = total
    rq[me] = prob
    keep = [terms(h, i, range(n)) for i in range(3)]
    partials[0].wait_recv()
    gate_out[...] = (keep[0] + dw_recv[0].astype(F32)).astype(BF16)

    for e in order[1:]:
        from_expert(e, 0).wait_recv()
        from_expert(e, 1).wait_recv()
    chosen = pick[...].reshape(n * block, 2 * rows)
    back_rows = mm(chosen, ret[...].reshape(n * block, ret.shape[2]), TN)
    act_out[...] = back_rows.astype(BF16).reshape(act_out.shape)
    back_prob = jnp.zeros((16, 2 * rows), F32)
    for e in range(n):
        back_prob = back_prob + mm(rq[e], pick[e], NN)
    prob_out[0:1, :] = back_prob[0:1, :rows].astype(BF16)
    prob_out[1:2, :] = back_prob[0:1, rows:].astype(BF16)

    partials[1].wait_recv()
    up_out[...] = (keep[1] + dw_recv[1].astype(F32)).astype(BF16)
    partials[2].wait_recv()
    down_out[...] = (keep[2] + dd_recv[...].astype(F32)).astype(BF16)

    for copy in weights + partials:
        copy.wait_send()
    for s in came:
        for which in range(4):
            forward(s, which, t).wait_send()
        for which in range(2):
            backward(s, which).wait_send()
    for e in order[1:]:
        for which in range(5):
            to_expert(e, which).wait_send()
        for which in range(2):
            to_source(e, which).wait_send()


def hand_over(*refs):
    copies = [pltpu.make_async_copy(refs[i], refs[5 + i], refs[10].at[i]) for i in range(5)]
    for copy in copies:
        copy.start()
    for copy in copies:
        copy.wait()


def on_device(acts, out_grad, probs, counts, w_gate, w_up, w_down):
    n = lax.axis_size("expert")
    pipes = lax.axis_size("pipe")
    rows, width = acts.shape[2], acts.shape[3]
    slots = 2 * rows // n
    block = 2 * slots
    deep, hidden = w_gate.shape[2], w_gate.shape[3]
    v = pltpu.VMEM
    dma = pltpu.SemaphoreType.DMA
    vmem = pl.BlockSpec(memory_space=pltpu.VMEM)
    hbm = pl.BlockSpec(memory_space=pl.ANY)
    outs = pl.pallas_call(
        functools.partial(kernel, n, pipes),
        out_shape=(
            jax.ShapeDtypeStruct((2, rows, width), BF16),
            jax.ShapeDtypeStruct((2, rows), BF16),
            jax.ShapeDtypeStruct((deep, hidden), BF16),
            jax.ShapeDtypeStruct((deep, hidden), BF16),
            jax.ShapeDtypeStruct((hidden, deep), BF16),
        ),
        in_specs=[vmem, vmem, vmem, pl.BlockSpec(memory_space=pltpu.SMEM), hbm, hbm, hbm],
        out_specs=(vmem,) * 5,
        scratch_shapes=[
            v((n, block, 2 * rows), BF16),
            v((n, block, width), BF16),
            v((n, block, width), BF16),
            v((n, 16, block), BF16),
            v((2, n, block, width), BF16),
            v((2, n, block, width), BF16),
            v((n, 16, block), BF16),
            v((2, deep, hidden), BF16),
            v((2, deep, hidden), BF16),
            v((2, hidden, deep), BF16),
            v((n, block, hidden), BF16),
            v((n, block, hidden), BF16),
            v((n, block, hidden), BF16),
            v((n, block, hidden), F32),
            v((n, block, hidden), F32),
            v((n, block, hidden), F32),
            v((2, deep, hidden), F32),
            v((hidden, deep), F32),
            v((n, block, width), F32),
            v((n, block, width), BF16),
            v((n, block, width), BF16),
            v((n, 8, block), F32),
            v((n, 8, block), F32),
            v((n, block, width), BF16),
            v((n, 16, block), BF16),
            v((n, block, width), BF16),
            v((n, 16, block), BF16),
            v((2, deep, hidden), BF16),
            v((hidden, deep), BF16),
            v((2, deep, hidden), BF16),
            v((hidden, deep), BF16),
            dma((7, n)),
            dma((7, n)),
            dma((4, n)),
            dma((4, n)),
            dma((2, n)),
            dma((2, n)),
            dma((3,)),
            dma((3,)),
            dma((3,)),
            dma((3,)),
            dma((3,)),
        ],
        compiler_params=pltpu.CompilerParams(
            collective_id=0, has_side_effects=True, vmem_limit_bytes=56 << 20
        ),
    )(acts[0], out_grad[0], probs[0], counts[0, :, 0, :], w_gate[0, 0], w_up[0, 0], w_down[0, 0])
    outs = pl.pallas_call(
        hand_over,
        out_shape=[jax.ShapeDtypeStruct(o.shape, o.dtype) for o in outs],
        in_specs=[vmem] * 5,
        out_specs=[hbm] * 5,
        scratch_shapes=[dma((5,))],
    )(*outs)
    return (outs[0][None], outs[1][None]) + tuple(o[None, None] for o in outs[2:])


def solution(mesh):
    return jax.shard_map(
        on_device,
        mesh=mesh,
        in_specs=(
            P("pipe", None, "expert", "tensor"),
            P("pipe", None, "expert", "tensor"),
            P("pipe", None, "expert"),
            P("pipe", None, "expert", None),
            P("pipe", "expert", None, "tensor"),
            P("pipe", "expert", None, "tensor"),
            P("pipe", "expert", "tensor", None),
        ),
        out_specs=(
            P("pipe", None, "expert", "tensor"),
            P("pipe", None, "expert"),
            P("pipe", "expert", None, "tensor"),
            P("pipe", "expert", None, "tensor"),
            P("pipe", "expert", "tensor", None),
        ),
        check_vma=False,
    )
```
